32 devices in a mesh: groups: 2 (over x), band: 16 (over z, y, core).
Axes of the slice: x: 2, y: 2, z: 4, core: 2. Of those that a mesh axis runs over, the one named last changes fastest.
Arguments:
- grid_rows: bfloat16 [16384, 1024], P(('groups', 'band')), parts along dimension 0, may hold values from -6 to 6
- row_slot: int32 [16384], P(('groups', 'band')), parts along dimension 0, may hold values from -1 to 511, as said below
- band_counts: int32 [32, 16], P('groups'), parts along dimension 0, may hold values from 1 to 32, as said below
- norm_gain: float32 [1024], replicated, may hold values from 0.1 to 1.9
- w_qkv: bfloat16 [1024, 3072], replicated
- w_out: bfloat16 [1024, 1024], replicated, may hold values from -0.1875 to 0.1875
Outputs:
- update: bfloat16 [16384, 1024], P(('groups', 'band')), parts along dimension 0
The draws below stay inside these ranges and needn't reach their ends.
There are 2 independent parts, one for each index of `groups`. The reference program is written for one: setup_inputs(seed, part) draws one part's arguments, and reference() takes and returns one part's arrays. A program takes and returns all parts, laid end to end along the dimension named above; an argument that names none is the same for every part. Nothing has to cross between parts.
Inputs may be any that keep to these rules, and one draw needn't show every extreme that they name: `row_slot`: values b * 32 + c of one owner's rows are distinct; the owner s holds exactly band_counts[s, b] rows with slots b * 32 + c, namely those with c < band_counts[s, b]; the other rows hold -1. `band_counts`: some band receives 32 rows from every owner.
All inputs are finite; a program needn't handle non-finite values.
Results may differ from the reference program's by a relative error of at most 0.009.
Values may be sent and summed in bfloat16 or wider, within the bound.
A program may use at most 64 MiB of HBM per device.

```python
import jax
import jax.numpy as jnp
from jax import lax

D = 1024
HEADS = 16
ROWS_DEV = 512
CAP = 32
WIN = 128
GRID = 8192
N_BAND = 16


def relay_tables(key):
    key = jax.random.fold_in(key, 11)
    first_key, second_key, third_key = jax.random.split(key, 3)
    position = jnp.arange(N_BAND, dtype=jnp.int32)
    lowest = CAP // 2
    reach = lowest + (CAP - lowest) * 2 * jnp.minimum(position, N_BAND - 1 - position) // max(N_BAND - 1, 1)
    reach = jnp.clip(reach, 1, CAP).astype(jnp.int32)
    raw_counts = jax.random.randint(first_key, (N_BAND, N_BAND), 0, 1 << 20, dtype=jnp.int32)
    counts = reach[None, :] - raw_counts % (reach[None, :] // 2 + 1)
    counts = jnp.clip(counts, 0, CAP)
    full_band = jax.random.randint(second_key, (), 0, N_BAND, dtype=jnp.int32)
    counts = jnp.where(position[None, :] == full_band, CAP, counts).astype(jnp.int32)
    slot_index = jnp.arange(ROWS_DEV, dtype=jnp.int32)
    live_slot = (slot_index % CAP)[None, :] < counts[:, slot_index // CAP]

    def per_source(live_row, source_key):
        order = jnp.argsort(1 - live_row.astype(jnp.int32), stable=True).astype(jnp.int32)
        number = jnp.sum(live_row.astype(jnp.int32))
        shuffle = jax.random.permutation(source_key, ROWS_DEV)
        assigned = jnp.where(slot_index < number, order, -1).astype(jnp.int32)
        return jnp.zeros((ROWS_DEV,), jnp.int32).at[shuffle].set(assigned)
    slots = jax.vmap(per_source)(live_slot, jax.random.split(third_key, N_BAND))
    return (counts, slots.reshape(-1))


def draw_row_slot(key, part):
    counts, slots = relay_tables(key)
    return slots


def draw_band_counts(key, part):
    counts, slots = relay_tables(key)
    return counts


def draw_w_qkv(key, part):
    key = jax.random.fold_in(key, 5)
    first_key = jax.random.fold_in(key, 0)
    result = jax.random.normal(first_key, (D, 3 * D), jnp.float32) * D ** (-0.5)
    return result.astype(jnp.bfloat16)


def steps_of(stream_key, shape, shards, smallest, largest):
    loudness = 1.0
    for dim, parts in shards:
        draws = jax.random.uniform(jax.random.fold_in(jax.random.fold_in(stream_key, 6), dim), (parts,), jnp.float32, smallest / len(shards), largest / len(shards))
        loudness = loudness * jnp.repeat(jnp.exp(draws), shape[dim] // parts).reshape((-1,) + (1,) * (len(shape) - 1 - dim))
    return loudness


def bell_draw(own_key, dims, scale, bound, cuts=(), kind=jnp.bfloat16):
    drawn = jax.random.normal(own_key, dims, jnp.float32) * scale
    if len(cuts) > 0:
        drawn = steps_of(own_key, dims, cuts, -0.22, 0.18) * drawn
    return jnp.clip(drawn, min=-bound, max=bound).astype(kind)


def setup_inputs(seed: int = 0, part: int = 0) -> dict:
    seeds = jax.random.split(jax.random.key(seed), 7)
    own_keys = jax.random.split(jax.random.fold_in(seeds[6], part), 7)
    return {
        "grid_rows": bell_draw(own_keys[0], (GRID, D), 1.0, 6.0, ((0, 16),)),
        "row_slot": draw_row_slot(jax.random.fold_in(jax.random.fold_in(seeds[6], part), 71), part),
        "band_counts": draw_band_counts(jax.random.fold_in(jax.random.fold_in(seeds[6], part), 71), part),
        "norm_gain": jnp.clip(1.0 + 0.18 * jax.random.normal(seeds[3], (D,), jnp.float32), 0.1, 1.9),
        "w_qkv": draw_w_qkv(jax.random.fold_in(seeds[6], 71), part),
        "w_out": bell_draw(seeds[5], (D, D), D ** -0.5, 0.1875),
    }


def normalize(rows_in, norm_gain):
    values = rows_in.astype(jnp.float32)
    center = lax.optimization_barrier(jnp.mean(values, axis=-1, keepdims=True))
    spread = lax.optimization_barrier(jnp.mean((values - center) ** 2, axis=-1, keepdims=True))
    return ((values - center) * lax.rsqrt(spread + 1e-05) * norm_gain).astype(jnp.bfloat16)

def attend(query, wide, key_alive, query_alive, w_out):
    row_count, feat_width = query.shape
    window = (wide.shape[0] - row_count) // 2
    head_dim = feat_width // HEADS
    group_count = HEADS // 4
    distance = jnp.arange(wide.shape[0], dtype=jnp.int32)[None, :] - window - jnp.arange(row_count, dtype=jnp.int32)[:, None]
    allowed = (jnp.abs(distance) <= window) & key_alive[None, :]
    queries = query.reshape(row_count, group_count, 4, head_dim).transpose(1, 0, 2, 3)
    keys = wide[:, :feat_width].reshape(-1, group_count, 4, head_dim).transpose(1, 0, 2, 3)
    values = wide[:, feat_width:].reshape(-1, group_count, 4, head_dim).transpose(1, 0, 2, 3)

    def one_group(operands):
        query_group, key_group, value_group = operands
        scores = jnp.einsum('qhd,khd->hqk', query_group.astype(jnp.float32), key_group.astype(jnp.float32)) * head_dim ** (-0.5)
        scores = jnp.where(allowed[None], scores, -1e+30)
        highest = lax.optimization_barrier(jnp.max(scores, axis=-1, keepdims=True))
        exponent = jnp.exp(scores - highest)
        weights = (exponent / lax.optimization_barrier(jnp.sum(exponent, axis=-1, keepdims=True))).astype(jnp.bfloat16)
        blended = jnp.einsum('hqk,khd->qhd', weights.astype(jnp.float32), value_group.astype(jnp.float32))
        return blended.astype(jnp.bfloat16)
    mixed = lax.map(one_group, (queries, keys, values))
    mixed = mixed.transpose(1, 0, 2, 3).reshape(row_count, feat_width)
    update = jnp.dot(mixed, w_out, preferred_element_type=jnp.float32)
    return jnp.where(query_alive[:, None], update, 0.0).astype(jnp.bfloat16)

def reference(grid_rows, row_slot, band_counts, norm_gain, w_qkv, w_out):
    total = GRID
    source = jnp.arange(total, dtype=jnp.int32) // ROWS_DEV
    target = jnp.where(row_slot >= 0, row_slot // CAP * ROWS_DEV + source * CAP + row_slot % CAP, total).astype(jnp.int32)
    mesh_rows = jnp.zeros((total + 1, D), jnp.bfloat16).at[target].set(grid_rows)[:total]
    position = jnp.arange(total, dtype=jnp.int32)
    band_of = position // ROWS_DEV
    owner_of = position % ROWS_DEV // CAP
    alive = position % CAP < band_counts[owner_of, band_of]
    normed = normalize(mesh_rows, norm_gain)
    qkv = jnp.dot(normed, w_qkv, preferred_element_type=jnp.float32).astype(jnp.bfloat16)
    keyval = jnp.concatenate([jnp.zeros((WIN, 2 * D), jnp.bfloat16), qkv[:, D:], jnp.zeros((WIN, 2 * D), jnp.bfloat16)], 0)
    alive_wide = jnp.concatenate([jnp.zeros((WIN,), bool), alive, jnp.zeros((WIN,), bool)], 0)

    def one_band(band_here):
        start = (band_here * ROWS_DEV).astype(jnp.int32)
        query = lax.dynamic_slice_in_dim(qkv[:, :D], start, ROWS_DEV, 0)
        wide = lax.dynamic_slice_in_dim(keyval, start, ROWS_DEV + 2 * WIN, 0)
        key_alive = lax.dynamic_slice_in_dim(alive_wide, start, ROWS_DEV + 2 * WIN, 0)
        query_alive = lax.dynamic_slice_in_dim(alive, start, ROWS_DEV, 0)
        return attend(query, wide, key_alive, query_alive, w_out)
    result = lax.map(one_band, jnp.arange(N_BAND, dtype=jnp.int32))
    return result.reshape(total, D)
```

```python
import functools
import math

import jax
import jax.numpy as jnp
from jax import lax
from jax.experimental import pallas as pl
from jax.experimental.pallas import tpu as pltpu
from jax.sharding import PartitionSpec as P

HEADS = 16
MASKED = -1e30
F32 = jnp.float32
BF16 = jnp.bfloat16


def kernel(
    bands, rows_hbm, slot_ref, counts_ref, gain_ref, wqkv_hbm, wout_hbm, out_ref,
    rows, wqkv, wout, outgoing, arrived, halo, normed, query, keyval, mixed,
    load_sem, send_sem, recv_sem, halo_send, halo_recv,
):
    row_count, width = rows.shape
    cap = row_count // bands
    block = row_count // 4
    per_block = block // cap
    head_dim = width // HEADS
    me = lax.axis_index("band")

    loads = [
        pltpu.make_async_copy(source, target, load_sem.at[i])
        for i, (source, target) in enumerate(((rows_hbm, rows), (wqkv_hbm, wqkv), (wout_hbm, wout)))
    ]
    loads[0].start()

    barrier = pltpu.get_barrier_semaphore()

    def greet(step, carry):
        pl.semaphore_signal(barrier, inc=1, device_id={"band": lax.rem(me + step, bands)})
        return carry

    lax.fori_loop(1, bands, greet, 0)
    loads[0].wait()
    loads[1].start()
    loads[2].start()

    for j in range(4):
        slot_of = lax.broadcasted_iota(jnp.int32, (block, row_count), 0) + j * block
        onehot = (slot_of == slot_ref[...]).astype(BF16)
        placed = jnp.dot(onehot, rows[...], preferred_element_type=F32)
        outgoing[pl.ds(j * per_block, per_block)] = placed.reshape(per_block, cap, width).astype(BF16)
    arrived[pl.ds(me, 1)] = outgoing[pl.ds(me, 1)]

    def chunk(target, slot):
        return pltpu.make_async_remote_copy(
            src_ref=outgoing.at[target],
            dst_ref=arrived.at[slot],
            send_sem=send_sem.at[target],
            recv_sem=recv_sem.at[slot],
            device_id={"band": target},
        )

    pl.semaphore_wait(barrier, bands - 1)

    def send(step, carry):
        half = lax.div(step, 2)
        shift = bands // 2 + half * (1 - 2 * lax.rem(step, 2))
        chunk(lax.rem(me + shift, bands), me).start()
        return carry

    lax.fori_loop(1, bands, send, 0)

    def wait_block(j):
        def one(owner, carry):
            @pl.when(owner != me)
            def _():
                chunk(owner, owner).wait_recv()
            return carry

        lax.fori_loop(j * per_block, (j + 1) * per_block, one, 0)

    def edge(side, peer):
        return pltpu.make_async_remote_copy(
            src_ref=arrived.at[pl.ds(0 if side == 0 else 3 * per_block, per_block)],
            dst_ref=halo.at[1 - side],
            send_sem=halo_send.at[side],
            recv_sem=halo_recv.at[1 - side],
            device_id={"band": peer},
        )

    def normalize(chunks, first):
        values = chunks.astype(F32).reshape(block, width)
        center = jnp.mean(values, axis=-1, keepdims=True)
        values = values - center
        spread = jnp.mean(values * values, axis=-1, keepdims=True)
        normed[pl.ds(first, block)] = (values * lax.rsqrt(spread + 1e-05) * gain_ref[...]).astype(BF16)

    has_prev, has_next = me > 0, me < bands - 1
    wait_block(0)

    @pl.when(has_prev)
    def _():
        edge(0, me - 1).start()

    wait_block(3)

    @pl.when(has_next)
    def _():
        edge(1, me + 1).start()

    normalize(arrived[pl.ds(0, per_block)], block)
    normalize(arrived[pl.ds(3 * per_block, per_block)], 4 * block)
    wait_block(1)
    normalize(arrived[pl.ds(per_block, per_block)], 2 * block)
    wait_block(2)
    normalize(arrived[pl.ds(2 * per_block, per_block)], 3 * block)
    loads[1].wait()

    tile = width // 2
    factor = head_dim ** -0.5 * math.log2(math.e)

    def project_query(c, carry):
        columns = pl.ds(pl.multiple_of(c * tile, tile), tile)
        part = jnp.dot(normed[pl.ds(block, row_count)], wqkv[:, columns], preferred_element_type=F32)
        query[:, columns] = (part * factor).astype(BF16)
        return carry

    def project_keyval(first, count):
        def one(c, carry):
            columns = pl.ds(pl.multiple_of(c * tile, tile), tile)
            source = pl.ds(pl.multiple_of(c * tile + width, tile), tile)
            keyval[pl.ds(first, count), columns] = jnp.dot(
                normed[pl.ds(first, count)], wqkv[:, source], preferred_element_type=F32
            ).astype(BF16)
            return carry

        lax.fori_loop(0, 4, one, 0)

    lax.fori_loop(0, 2, project_query, 0)
    project_keyval(block, row_count)

    for side, there, peer in ((0, has_prev, me - 1), (1, has_next, me + 1)):
        @pl.when(there)
        def _(side=side, peer=peer):
            edge(1 - side, peer).wait_recv()

        @pl.when(jnp.logical_not(there))
        def _(side=side):
            halo[side] = jnp.zeros(halo.shape[1:], BF16)

        first = side * 5 * block
        normalize(halo[side], first)
        project_keyval(first, block)

    wide_count = row_count + 2 * block
    counts = counts_ref[...].astype(F32)
    band_lane = lax.broadcasted_iota(jnp.int32, (bands, bands), 1)

    def alive_row(band, owner_first, count):
        column = jnp.sum(jnp.where(band_lane == band, counts, 0.0), axis=1, keepdims=True)
        position = lax.broadcasted_iota(jnp.int32, (bands, count), 1) + owner_first * cap
        owner = lax.broadcasted_iota(jnp.int32, (bands, count), 0)
        here = jnp.sum(jnp.where(position // cap == owner, column, 0.0), axis=0, keepdims=True)
        number = (lax.broadcasted_iota(jnp.int32, (1, count), 1) % cap).astype(F32)
        return jnp.where(number < here, 0.0, MASKED)

    key_bias = jnp.concatenate(
        [alive_row(me - 1, 3 * per_block, block), alive_row(me, 0, row_count), alive_row(me + 1, 0, block)], axis=1
    )
    lane = lax.broadcasted_iota(jnp.int32, (1, 2 * head_dim), 1)
    first_head = lane < head_dim
    masks = [jnp.where(first_head, 1.0, 0.0).astype(BF16), jnp.where(first_head, 0.0, 1.0).astype(BF16)]
    key_at = lax.broadcasted_iota(jnp.int32, (block, 3 * block), 1)
    query_at = lax.broadcasted_iota(jnp.int32, (block, 3 * block), 0)
    within = (key_at >= query_at) & (key_at <= query_at + 2 * block)
    loads[2].wait()
    owner_of = lax.broadcasted_iota(jnp.int32, (block, bands), 0) // cap
    owner_lane = lax.broadcasted_iota(jnp.int32, (block, bands), 1)
    for j in range(4):
        queries = pl.ds(j * block, block)
        keys = pl.ds(j * block, 3 * block)
        bias = jnp.where(within, key_bias[:, j * block:(j + 3) * block], MASKED)

        def pair_of_heads(p, carry, queries=queries, keys=keys, bias=bias):
            columns = pl.ds(pl.multiple_of(p * 2 * head_dim, 2 * head_dim), 2 * head_dim)
            value_columns = pl.ds(pl.multiple_of(width + p * 2 * head_dim, 2 * head_dim), 2 * head_dim)
            both = query[queries, columns]
            stacked = jnp.concatenate([both * masks[0], both * masks[1]], axis=0)
            score = lax.dot_general(
                stacked, keyval[keys, columns], (((1,), (1,)), ((), ())), preferred_element_type=F32
            )
            score = score.reshape(2, block, 3 * block) + bias[None]
            weight = jnp.exp2(score - jnp.max(score, axis=-1, keepdims=True))
            total = jnp.sum(weight, axis=-1, keepdims=True)
            blended = jnp.dot(
                weight.reshape(2 * block, 3 * block).astype(BF16), keyval[keys, value_columns],
                preferred_element_type=F32,
            ).reshape(2, block, 2 * head_dim) / total
            mixed[:, columns] = jnp.where(first_head, blended[0], blended[1]).astype(BF16)
            return carry

        lax.fori_loop(0, HEADS // 2, pair_of_heads, 0, unroll=True)
        update = jnp.dot(mixed[...], wout[...], preferred_element_type=F32)
        spread_counts = jnp.dot(
            (owner_of + j * per_block == owner_lane).astype(F32), counts, preferred_element_type=F32
        )
        column = jnp.sum(jnp.where(owner_lane == me, spread_counts, 0.0), axis=1, keepdims=True)
        number = (lax.broadcasted_iota(jnp.int32, (block, 1), 0) % cap).astype(F32)
        out_ref[queries, :] = jnp.where(number < column, update, 0.0).astype(BF16)

    def sent(step, carry):
        chunk(lax.rem(me + step, bands), me).wait_send()
        return carry

    lax.fori_loop(1, bands, sent, 0)

    @pl.when(has_prev)
    def _():
        edge(0, me - 1).wait_send()

    @pl.when(has_next)
    def _():
        edge(1, me + 1).wait_send()


def body(grid_rows, row_slot, band_counts, norm_gain, w_qkv, w_out):
    row_count, width = grid_rows.shape
    bands = lax.axis_size("band")
    cap = row_count // bands
    block = row_count // 4
    vmem = pl.BlockSpec(memory_space=pltpu.VMEM)
    anywhere = pl.BlockSpec(memory_space=pl.ANY)
    return pl.pallas_call(
        functools.partial(kernel, bands),
        out_shape=jax.ShapeDtypeStruct((row_count, width), BF16),
        in_specs=[anywhere, vmem, vmem, vmem, anywhere, anywhere],
        out_specs=vmem,
        scratch_shapes=[
            pltpu.VMEM((row_count, width), BF16),
            pltpu.VMEM(w_qkv.shape, BF16),
            pltpu.VMEM(w_out.shape, BF16),
            pltpu.VMEM((bands, cap, width), BF16),
            pltpu.VMEM((bands, cap, width), BF16),
            pltpu.VMEM((2, block // cap, cap, width), BF16),
            pltpu.VMEM((row_count + 2 * block, width), BF16),
            pltpu.VMEM((row_count, width), BF16),
            pltpu.VMEM((row_count + 2 * block, 2 * width), BF16),
            pltpu.VMEM((block, width), BF16),
            pltpu.SemaphoreType.DMA((3,)),
            pltpu.SemaphoreType.DMA((bands,)),
            pltpu.SemaphoreType.DMA((bands,)),
            pltpu.SemaphoreType.DMA((2,)),
            pltpu.SemaphoreType.DMA((2,)),
        ],
        compiler_params=pltpu.CompilerParams(
            collective_id=0, has_side_effects=True, vmem_limit_bytes=48 * 1024 * 1024
        ),
    )(grid_rows, row_slot.reshape(1, row_count), band_counts, norm_gain.reshape(1, width), w_qkv, w_out)


def solution(mesh):
    return jax.shard_map(
        body,
        mesh=mesh,
        in_specs=(
            P(("groups", "band"), None),
            P(("groups", "band")),
            P("groups", None),
            P(),
            P(),
            P(),
        ),
        out_specs=P(("groups", "band"), None),
        check_vma=False,
    )
```

```python
import functools
import math

import jax
import jax.numpy as jnp
from jax import lax
from jax.experimental import pallas as pl
from jax.experimental.pallas import tpu as pltpu
from jax.sharding import PartitionSpec as P

HEADS = 16
MASKED = -1e30
F32 = jnp.float32
BF16 = jnp.bfloat16


def kernel(
    bands, rows_hbm, slot_hbm, counts_hbm, gain_hbm, wqkv_hbm, wout_hbm, out_ref,
    rows, slot_ref, counts_ref, gain_ref, wqkv, wout, outgoing, arrived, halo, normed, query, keyval, mixed,
    load_sem, send_sem, recv_sem, halo_send, halo_recv,
):
    row_count, width = rows.shape
    cap = row_count // bands
    block = row_count // 4
    per_block = block // cap
    head_dim = width // HEADS
    me = lax.axis_index("band")

    loads = [
        pltpu.make_async_copy(source, target, load_sem.at[i])
        for i, (source, target) in enumerate((
            (slot_hbm, slot_ref), (rows_hbm, rows), (gain_hbm, gain_ref), (counts_hbm, counts_ref),
            (wqkv_hbm, wqkv), (wout_hbm, wout),
        ))
    ]
    for load in loads:
        load.start()

    barrier = pltpu.get_barrier_semaphore()

    def greet(step, carry):
        pl.semaphore_signal(barrier, inc=1, device_id={"band": lax.rem(me + step, bands)})
        return carry

    lax.fori_loop(1, bands, greet, 0)
    loads[0].wait()
    loads[1].wait()

    quarter = me // per_block
    ascending = quarter % 2 == 1

    def chunk(target, slot):
        return pltpu.make_async_remote_copy(
            src_ref=outgoing.at[target],
            dst_ref=arrived.at[slot],
            send_sem=send_sem.at[target],
            recv_sem=recv_sem.at[slot],
            device_id={"band": target},
        )

    for step in range(4):
        part = jnp.where(ascending, step, 3 - step)
        slot_of = lax.broadcasted_iota(jnp.int32, (block, row_count), 0) + part * block
        onehot = (slot_of == slot_ref[...]).astype(BF16)
        placed = jnp.dot(onehot, rows[...], preferred_element_type=F32)
        outgoing[pl.ds(part * per_block, per_block)] = placed.reshape(per_block, cap, width).astype(BF16)
        if step == 0:
            pl.semaphore_wait(barrier, bands - 1)

        def send(i, carry, part=part):
            target = part * per_block + (me + i) % per_block

            @pl.when(target != me)
            def _():
                chunk(target, me).start()

            return carry

        lax.fori_loop(0, per_block, send, 0)
    arrived[pl.ds(me, 1)] = outgoing[pl.ds(me, 1)]

    def wait_block(j):
        def one(i, carry):
            owner = j * per_block + i

            @pl.when(owner != me)
            def _():
                chunk(owner, owner).wait_recv()
            return carry

        lax.fori_loop(0, per_block, one, 0)

    def edge(side, peer):
        return pltpu.make_async_remote_copy(
            src_ref=arrived.at[pl.ds(0 if side == 0 else 3 * per_block, per_block)],
            dst_ref=halo.at[1 - side],
            send_sem=halo_send.at[side],
            recv_sem=halo_recv.at[1 - side],
            device_id={"band": peer},
        )

    def normalize(chunks, place):
        values = chunks.astype(F32).reshape(block, width)
        center = jnp.mean(values, axis=-1, keepdims=True)
        values = values - center
        spread = jnp.mean(values * values, axis=-1, keepdims=True)
        normed[pl.ds(place * block, block)] = (values * lax.rsqrt(spread + 1e-05) * gain_ref[...]).astype(BF16)

    tile = width // 2
    factor = head_dim ** -0.5 * math.log2(math.e)

    def project_query(place, count, blocks):
        def one(c, carry):
            columns = pl.ds(pl.multiple_of(c * tile, tile), tile)
            part = jnp.dot(normed[pl.ds(place * block, count * block)], wqkv[:, columns], preferred_element_type=F32)
            part = (part * factor).astype(BF16)
            for i, at in enumerate(blocks):
                query[pl.ds(pl.multiple_of(at * block, block), block), columns] = part[i * block:(i + 1) * block]
            return carry

        lax.fori_loop(0, 2, one, 0)

    def project_keyval(place, count, blocks):
        def one(c, carry):
            columns = pl.ds(pl.multiple_of(c * tile, tile), tile)
            source = pl.ds(pl.multiple_of(c * tile + width, tile), tile)
            part = jnp.dot(normed[pl.ds(place * block, count * block)], wqkv[:, source], preferred_element_type=F32)
            part = part.astype(BF16)
            for i, at in enumerate(blocks):
                keyval[pl.ds(pl.multiple_of((at + 1) * block, block), block), columns] = part[i * block:(i + 1) * block]
            return carry

        lax.fori_loop(0, 4, one, 0)

    upper = quarter // 2
    near_inner, near_outer = 1 + upper, 3 * upper
    far_outer, far_inner = 3 - 3 * upper, 2 - upper
    has_prev, has_next = me > 0, me < bands - 1

    def arrived_block(j):
        return arrived[pl.ds(j * per_block, per_block)]

    def pass_on(j):
        @pl.when((j == 0) & has_prev)
        def _():
            edge(0, me - 1).start()

        @pl.when((j == 3) & has_next)
        def _():
            edge(1, me + 1).start()

    loads[2].wait()
    loads[3].wait()
    loads[4].wait()
    wait_block(near_inner)
    normalize(arrived_block(near_inner), 0)
    project_query(0, 1, (near_inner,))
    project_keyval(0, 1, (near_inner,))
    wait_block(near_outer)
    pass_on(near_outer)
    wait_block(far_outer)
    pass_on(far_outer)
    normalize(arrived_block(near_outer), 1)
    normalize(arrived_block(far_outer), 2)
    project_query(1, 2, (near_outer, far_outer))
    project_keyval(1, 2, (near_outer, far_outer))
    for side, there, peer in ((0, has_prev, me - 1), (1, has_next, me + 1)):
        @pl.when(there)
        def _(side=side, peer=peer):
            edge(1 - side, peer).wait_recv()

        @pl.when(jnp.logical_not(there))
        def _(side=side):
            halo[side] = jnp.zeros(halo.shape[1:], BF16)

        normalize(halo[side], 3 + side)
    wait_block(far_inner)
    normalize(arrived_block(far_inner), 5)
    project_query(5, 1, (far_inner,))
    project_keyval(3, 3, (-1, 4, far_inner))

    wide_count = row_count + 2 * block
    counts = counts_ref[...].astype(F32)
    band_lane = lax.broadcasted_iota(jnp.int32, (bands, bands), 1)

    def alive_row(band, owner_first, count):
        column = jnp.sum(jnp.where(band_lane == band, counts, 0.0), axis=1, keepdims=True)
        position = lax.broadcasted_iota(jnp.int32, (bands, count), 1) + owner_first * cap
        owner = lax.broadcasted_iota(jnp.int32, (bands, count), 0)
        here = jnp.sum(jnp.where(position // cap == owner, column, 0.0), axis=0, keepdims=True)
        number = (lax.broadcasted_iota(jnp.int32, (1, count), 1) % cap).astype(F32)
        return jnp.where(number < here, 0.0, MASKED)

    key_bias = jnp.concatenate(
        [alive_row(me - 1, 3 * per_block, block), alive_row(me, 0, row_count), alive_row(me + 1, 0, block)], axis=1
    )
    lane = lax.broadcasted_iota(jnp.int32, (1, 2 * head_dim), 1)
    first_head = lane < head_dim
    masks = [jnp.where(first_head, 1.0, 0.0).astype(BF16), jnp.where(first_head, 0.0, 1.0).astype(BF16)]
    key_at = lax.broadcasted_iota(jnp.int32, (block, 3 * block), 1)
    query_at = lax.broadcasted_iota(jnp.int32, (block, 3 * block), 0)
    within = (key_at >= query_at) & (key_at <= query_at + 2 * block)
    loads[5].wait()
    owner_of = lax.broadcasted_iota(jnp.int32, (block, bands), 0) // cap
    owner_lane = lax.broadcasted_iota(jnp.int32, (block, bands), 1)
    for j in range(4):
        queries = pl.ds(j * block, block)
        keys = pl.ds(j * block, 3 * block)
        bias = jnp.where(within, key_bias[:, j * block:(j + 3) * block], MASKED)

        def score_of(p, queries=queries, keys=keys):
            columns = slice(p * 2 * head_dim, (p + 1) * 2 * head_dim)
            key = keyval[keys, columns]
            return lax.dot_general(
                query[queries, columns], jnp.concatenate([key * masks[0], key * masks[1]], axis=0),
                (((1,), (1,)), ((), ())), preferred_element_type=F32,
            )

        score = score_of(0)
        for p in range(HEADS // 2):
            later = score_of(p + 1) if p + 1 < HEADS // 2 else None
            weights = []
            for h in range(2):
                own = score[:, h * 3 * block:(h + 1) * 3 * block] + bias
                weights.append(jnp.exp2(own - jnp.max(own, axis=-1, keepdims=True)).astype(BF16))
            value = keyval[keys, width + p * 2 * head_dim:width + (p + 1) * 2 * head_dim]
            blended = jnp.dot(
                jnp.concatenate(weights, axis=1),
                jnp.concatenate([
                    jnp.concatenate([value * mask, jnp.broadcast_to(mask, value.shape)], axis=1) for mask in masks
                ], axis=0),
                preferred_element_type=F32,
            )
            mixed[:, p * 2 * head_dim:(p + 1) * 2 * head_dim] = (
                blended[:, :2 * head_dim] / blended[:, 2 * head_dim:]
            ).astype(BF16)
            score = later

        update = jnp.dot(mixed[...], wout[...], preferred_element_type=F32)
        spread_counts = jnp.dot(
            (owner_of + j * per_block == owner_lane).astype(F32), counts, preferred_element_type=F32
        )
        column = jnp.sum(jnp.where(owner_lane == me, spread_counts, 0.0), axis=1, keepdims=True)
        number = (lax.broadcasted_iota(jnp.int32, (block, 1), 0) % cap).astype(F32)
        out_ref[queries, :] = jnp.where(number < column, update, 0.0).astype(BF16)

    def sent(step, carry):
        chunk(lax.rem(me + step, bands), me).wait_send()
        return carry

    lax.fori_loop(1, bands, sent, 0)

    @pl.when(has_prev)
    def _():
        edge(0, me - 1).wait_send()

    @pl.when(has_next)
    def _():
        edge(1, me + 1).wait_send()


def body(grid_rows, row_slot, band_counts, norm_gain, w_qkv, w_out):
    row_count, width = grid_rows.shape
    bands = lax.axis_size("band")
    cap = row_count // bands
    block = row_count // 4
    vmem = pl.BlockSpec(memory_space=pltpu.VMEM)
    hbm = pl.BlockSpec(memory_space=pltpu.HBM)
    return pl.pallas_call(
        functools.partial(kernel, bands),
        out_shape=jax.ShapeDtypeStruct((row_count, width), BF16),
        in_specs=[hbm] * 6,
        out_specs=vmem,
        scratch_shapes=[
            pltpu.VMEM((row_count, width), BF16),
            pltpu.VMEM((1, row_count), jnp.int32),
            pltpu.VMEM((bands, bands), jnp.int32),
            pltpu.VMEM((1, width), F32),
            pltpu.VMEM(w_qkv.shape, BF16),
            pltpu.VMEM(w_out.shape, BF16),
            pltpu.VMEM((bands, cap, width), BF16),
            pltpu.VMEM((bands, cap, width), BF16),
            pltpu.VMEM((2, block // cap, cap, width), BF16),
            pltpu.VMEM((row_count + 2 * block, width), BF16),
            pltpu.VMEM((row_count, width), BF16),
            pltpu.VMEM((row_count + 2 * block, 2 * width), BF16),
            pltpu.VMEM((block, width), BF16),
            pltpu.SemaphoreType.DMA((6,)),
            pltpu.SemaphoreType.DMA((bands,)),
            pltpu.SemaphoreType.DMA((bands,)),
            pltpu.SemaphoreType.DMA((2,)),
            pltpu.SemaphoreType.DMA((2,)),
        ],
        compiler_params=pltpu.CompilerParams(
            collective_id=0, has_side_effects=True, vmem_limit_bytes=64 * 1024 * 1024
        ),
    )(grid_rows, row_slot.reshape(1, row_count), band_counts, norm_gain.reshape(1, width), w_qkv, w_out)


def solution(mesh):
    return jax.shard_map(
        body,
        mesh=mesh,
        in_specs=(
            P(("groups", "band"), None),
            P(("groups", "band")),
            P("groups", None),
            P(),
            P(),
            P(),
        ),
        out_specs=P(("groups", "band"), None),
        check_vma=False,
    )
```

```python
import functools
import math

import jax
import jax.numpy as jnp
from jax import lax
from jax.experimental import pallas as pl
from jax.experimental.pallas import tpu as pltpu
from jax.sharding import PartitionSpec as P

HEADS = 16
MASKED = -1e30
F32 = jnp.float32
BF16 = jnp.bfloat16


def kernel(
    bands, rows_hbm, slot_hbm, counts_hbm, gain_hbm, wqkv_hbm, wout_hbm, out_ref,
    rows, slot_ref, counts_ref, gain_ref, wqkv, wout, outgoing, arrived, halo, normed, query, keyval, mixed,
    load_sem, send_sem, recv_sem, halo_send, halo_recv,
):
    row_count, width = rows.shape
    cap = row_count // bands
    block = row_count // 4
    per_block = block // cap
    head_dim = width // HEADS
    me = lax.axis_index("band")

    loads = [
        pltpu.make_async_copy(source, target, load_sem.at[i])
        for i, (source, target) in enumerate((
            (slot_hbm, slot_ref), (rows_hbm, rows), (gain_hbm, gain_ref), (counts_hbm, counts_ref),
            (wqkv_hbm, wqkv), (wout_hbm, wout),
        ))
    ]
    for load in loads:
        load.start()

    barrier = pltpu.get_barrier_semaphore()

    def greet(step, carry):
        pl.semaphore_signal(barrier, inc=1, device_id={"band": lax.rem(me + step, bands)})
        return carry

    lax.fori_loop(1, bands, greet, 0)
    loads[0].wait()
    loads[1].wait()

    quarter = me // per_block
    ascending = quarter % 2 == 1

    def chunk(target, slot):
        return pltpu.make_async_remote_copy(
            src_ref=outgoing.at[target],
            dst_ref=arrived.at[slot],
            send_sem=send_sem.at[target],
            recv_sem=recv_sem.at[slot],
            device_id={"band": target},
        )

    for step in range(4):
        part = jnp.where(ascending, step, 3 - step)
        slot_of = lax.broadcasted_iota(jnp.int32, (block, row_count), 0) + part * block
        onehot = (slot_of == slot_ref[...]).astype(BF16)
        placed = jnp.dot(onehot, rows[...], preferred_element_type=F32)
        outgoing[pl.ds(part * per_block, per_block)] = placed.reshape(per_block, cap, width).astype(BF16)
        if step == 0:
            pl.semaphore_wait(barrier, bands - 1)

        def send(i, carry, part=part):
            target = part * per_block + (me + i) % per_block

            @pl.when(target != me)
            def _():
                chunk(target, me).start()

            return carry

        lax.fori_loop(0, per_block, send, 0)
    arrived[pl.ds(me, 1)] = outgoing[pl.ds(me, 1)]

    def edge(side, i, peer):
        return pltpu.make_async_remote_copy(
            src_ref=arrived.at[(0 if side == 0 else 3 * per_block) + i],
            dst_ref=halo.at[1 - side, i],
            send_sem=halo_send.at[side, i],
            recv_sem=halo_recv.at[1 - side, i],
            device_id={"band": peer},
        )

    def normalize(chunks, place):
        values = chunks.astype(F32).reshape(block, width)
        center = jnp.mean(values, axis=-1, keepdims=True)
        values = values - center
        spread = jnp.mean(values * values, axis=-1, keepdims=True)
        normed[pl.ds(place * block, block)] = (values * lax.rsqrt(spread + 1e-05) * gain_ref[...]).astype(BF16)

    tile = width // 2
    factor = head_dim ** -0.5 * math.log2(math.e)

    def project_query(place, count, blocks):
        def one(c, carry):
            columns = pl.ds(pl.multiple_of(c * tile, tile), tile)
            part = jnp.dot(normed[pl.ds(place * block, count * block)], wqkv[:, columns], preferred_element_type=F32)
            part = (part * factor).astype(BF16)
            for i, at in enumerate(blocks):
                query[pl.ds(pl.multiple_of(at * block, block), block), columns] = part[i * block:(i + 1) * block]
            return carry

        lax.fori_loop(0, 2, one, 0)

    def project_keyval(place, count, blocks):
        def one(c, carry):
            columns = pl.ds(pl.multiple_of(c * tile, tile), tile)
            source = pl.ds(pl.multiple_of(c * tile + width, tile), tile)
            part = jnp.dot(normed[pl.ds(place * block, count * block)], wqkv[:, source], preferred_element_type=F32)
            part = part.astype(BF16)
            for i, at in enumerate(blocks):
                keyval[pl.ds(pl.multiple_of((at + 1) * block, block), block), columns] = part[i * block:(i + 1) * block]
            return carry

        lax.fori_loop(0, 4, one, 0)

    upper = quarter // 2
    near_inner, near_outer = 1 + upper, 3 * upper
    far_outer, far_inner = 3 - 3 * upper, 2 - upper
    has_prev, has_next = me > 0, me < bands - 1

    def arrived_block(j):
        return arrived[pl.ds(j * per_block, per_block)]

    def wait_block(j, pass_on=False):
        def one(i, carry):
            owner = j * per_block + i

            @pl.when(owner != me)
            def _():
                chunk(owner, owner).wait_recv()

            if pass_on:
                @pl.when((j == 0) & has_prev)
                def _():
                    edge(0, i, me - 1).start()

                @pl.when((j == 3) & has_next)
                def _():
                    edge(1, i, me + 1).start()

            return carry

        lax.fori_loop(0, per_block, one, 0)

    def each_edge(act):
        lax.fori_loop(0, per_block, lambda i, carry: (act(i), carry)[1], 0)

    loads[2].wait()
    loads[3].wait()
    loads[4].wait()
    wait_block(near_inner)
    normalize(arrived_block(near_inner), 0)
    project_query(0, 1, (near_inner,))
    project_keyval(0, 1, (near_inner,))
    wait_block(near_outer, pass_on=True)
    wait_block(far_outer, pass_on=True)
    normalize(arrived_block(near_outer), 1)
    normalize(arrived_block(far_outer), 2)
    project_query(1, 2, (near_outer, far_outer))
    project_keyval(1, 2, (near_outer, far_outer))
    wait_block(far_inner)
    normalize(arrived_block(far_inner), 5)
    project_query(5, 1, (far_inner,))
    project_keyval(5, 1, (far_inner,))
    for side, there, peer in ((0, has_prev, me - 1), (1, has_next, me + 1)):
        @pl.when(there)
        def _(side=side, peer=peer):
            each_edge(lambda i: edge(1 - side, i, peer).wait_recv())

        @pl.when(jnp.logical_not(there))
        def _(side=side):
            halo[side] = jnp.zeros(halo.shape[1:], BF16)

        normalize(halo[side], 3 + side)
    project_keyval(3, 2, (-1, 4))

    wide_count = row_count + 2 * block
    counts = counts_ref[...].astype(F32)
    band_lane = lax.broadcasted_iota(jnp.int32, (bands, bands), 1)

    def alive_row(band, owner_first, count):
        column = jnp.sum(jnp.where(band_lane == band, counts, 0.0), axis=1, keepdims=True)
        position = lax.broadcasted_iota(jnp.int32, (bands, count), 1) + owner_first * cap
        owner = lax.broadcasted_iota(jnp.int32, (bands, count), 0)
        here = jnp.sum(jnp.where(position // cap == owner, column, 0.0), axis=0, keepdims=True)
        number = (lax.broadcasted_iota(jnp.int32, (1, count), 1) % cap).astype(F32)
        return jnp.where(number < here, 0.0, MASKED)

    key_bias = jnp.concatenate(
        [alive_row(me - 1, 3 * per_block, block), alive_row(me, 0, row_count), alive_row(me + 1, 0, block)], axis=1
    )
    lane = lax.broadcasted_iota(jnp.int32, (1, 2 * head_dim), 1)
    first_head = lane < head_dim
    masks = [jnp.where(first_head, 1.0, 0.0).astype(BF16), jnp.where(first_head, 0.0, 1.0).astype(BF16)]
    key_at = lax.broadcasted_iota(jnp.int32, (block, 3 * block), 1)
    query_at = lax.broadcasted_iota(jnp.int32, (block, 3 * block), 0)
    within = (key_at >= query_at) & (key_at <= query_at + 2 * block)
    loads[5].wait()
    owner_of = lax.broadcasted_iota(jnp.int32, (block, bands), 0) // cap
    owner_lane = lax.broadcasted_iota(jnp.int32, (block, bands), 1)
    alive = []
    for j in range(4):
        queries = pl.ds(j * block, block)
        keys = pl.ds(j * block, 3 * block)
        bias = jnp.where(within, key_bias[:, j * block:(j + 3) * block], MASKED)

        def score_of(p, queries=queries, keys=keys):
            columns = slice(p * 2 * head_dim, (p + 1) * 2 * head_dim)
            key = keyval[keys, columns]
            return lax.dot_general(
                query[queries, columns], jnp.concatenate([key * masks[0], key * masks[1]], axis=0),
                (((1,), (1,)), ((), ())), preferred_element_type=F32,
            )

        score = score_of(0)
        for p in range(HEADS // 2):
            later = score_of(p + 1) if p + 1 < HEADS // 2 else None
            weights = []
            for h in range(2):
                own = score[:, h * 3 * block:(h + 1) * 3 * block] + bias
                weights.append(jnp.exp2(own - jnp.max(own, axis=-1, keepdims=True)).astype(BF16))
            value = keyval[keys, width + p * 2 * head_dim:width + (p + 1) * 2 * head_dim]
            blended = jnp.dot(
                jnp.concatenate(weights, axis=1),
                jnp.concatenate([
                    jnp.concatenate([value * mask, jnp.broadcast_to(mask, value.shape)], axis=1) for mask in masks
                ], axis=0),
                preferred_element_type=F32,
            )
            mixed[queries, p * 2 * head_dim:(p + 1) * 2 * head_dim] = (
                blended[:, :2 * head_dim] / blended[:, 2 * head_dim:]
            ).astype(BF16)
            score = later

        spread_counts = jnp.dot(
            (owner_of + j * per_block == owner_lane).astype(F32), counts, preferred_element_type=F32
        )
        column = jnp.sum(jnp.where(owner_lane == me, spread_counts, 0.0), axis=1, keepdims=True)
        number = (lax.broadcasted_iota(jnp.int32, (block, 1), 0) % cap).astype(F32)
        alive.append(number < column)

    for c in range(2):
        columns = slice(c * tile, (c + 1) * tile)
        update = jnp.dot(mixed[...], wout[:, columns], preferred_element_type=F32)
        for j in range(4):
            queries = slice(j * block, (j + 1) * block)
            out_ref[queries, columns] = jnp.where(alive[j], update[queries], 0.0).astype(BF16)

    def sent(step, carry):
        chunk(lax.rem(me + step, bands), me).wait_send()
        return carry

    lax.fori_loop(1, bands, sent, 0)

    @pl.when(has_prev)
    def _():
        each_edge(lambda i: edge(0, i, me - 1).wait_send())

    @pl.when(has_next)
    def _():
        each_edge(lambda i: edge(1, i, me + 1).wait_send())


def body(grid_rows, row_slot, band_counts, norm_gain, w_qkv, w_out):
    row_count, width = grid_rows.shape
    bands = lax.axis_size("band")
    cap = row_count // bands
    block = row_count // 4
    vmem = pl.BlockSpec(memory_space=pltpu.VMEM)
    hbm = pl.BlockSpec(memory_space=pltpu.HBM)
    return pl.pallas_call(
        functools.partial(kernel, bands),
        out_shape=jax.ShapeDtypeStruct((row_count, width), BF16),
        in_specs=[hbm] * 6,
        out_specs=vmem,
        scratch_shapes=[
            pltpu.VMEM((row_count, width), BF16),
            pltpu.VMEM((1, row_count), jnp.int32),
            pltpu.VMEM((bands, bands), jnp.int32),
            pltpu.VMEM((1, width), F32),
            pltpu.VMEM(w_qkv.shape, BF16),
            pltpu.VMEM(w_out.shape, BF16),
            pltpu.VMEM((bands, cap, width), BF16),
            pltpu.VMEM((bands, cap, width), BF16),
            pltpu.VMEM((2, block // cap, cap, width), BF16),
            pltpu.VMEM((row_count + 2 * block, width), BF16),
            pltpu.VMEM((row_count, width), BF16),
            pltpu.VMEM((row_count + 2 * block, 2 * width), BF16),
            pltpu.VMEM((row_count, width), BF16),
            pltpu.SemaphoreType.DMA((6,)),
            pltpu.SemaphoreType.DMA((bands,)),
            pltpu.SemaphoreType.DMA((bands,)),
            pltpu.SemaphoreType.DMA((2, block // cap)),
            pltpu.SemaphoreType.DMA((2, block // cap)),
        ],
        compiler_params=pltpu.CompilerParams(
            collective_id=0, has_side_effects=True, vmem_limit_bytes=64 * 1024 * 1024
        ),
    )(grid_rows, row_slot.reshape(1, row_count), band_counts, norm_gain.reshape(1, width), w_qkv, w_out)


def solution(mesh):
    return jax.shard_map(
        body,
        mesh=mesh,
        in_specs=(
            P(("groups", "band"), None),
            P(("groups", "band")),
            P("groups", None),
            P(),
            P(),
            P(),
        ),
        out_specs=P(("groups", "band"), None),
        check_vma=False,
    )
```
